32 devices in a mesh: row: 32 (over z, y, x, core), col: 1.
Axes of the slice: x: 2, y: 2, z: 4, core: 2. Of those that a mesh axis runs over, the one named last changes fastest.
Arguments:
- left_factors: bfloat16 [1536, 32, 512], P('col', None, 'row'), may hold values from -0.15625 to 0.15625
- right_factors: bfloat16 [1536, 4, 512], P('col'), may hold values from -0.15625 to 0.15625
- amplitudes: bfloat16 [64, 512, 512], P('col', 'row'), may hold values from -0.46875 to 0.46875
Outputs:
- ladder: float32 [64, 32, 4], P('col', 'row')
The draws below stay inside these ranges and needn't reach their ends.
All inputs are finite; a program needn't handle non-finite values.
Results may differ from the reference program's by a relative error of at most 0.0029.
Values may be sent and summed in bfloat16 or wider, within the bound.
A program may use at most 64 MiB of HBM per device.

```python
import jax
import jax.numpy as jnp

V = 512
NAUX = 1536
NB = 4
NA = 32
NPAIR = 64


def steps_of(own_key, dims, cuts, least, top_value):
    loudness = 1.0
    for dim, shards_of in cuts:
        heights = jax.random.uniform(jax.random.fold_in(jax.random.fold_in(own_key, 6), dim), (shards_of,), jnp.float32, least / len(cuts), top_value / len(cuts))
        loudness = loudness * jnp.repeat(jnp.exp(heights), dims[dim] // shards_of).reshape((-1,) + (1,) * (len(dims) - 1 - dim))
    return loudness


def normal_values(key, dims, width, bound, split=(), kind=jnp.bfloat16):
    drawn = width * jax.random.normal(key, dims, jnp.float32)
    if split:
        drawn = drawn * steps_of(key, dims, split, -0.22, 0.18)
    return jnp.clip(drawn, -bound, bound).astype(kind)


def setup_inputs(seed: int = 0) -> dict:
    streams_of = jax.random.split(jax.random.key(seed), 4)
    left_factors = normal_values(streams_of[0], (NAUX, NA, V), NAUX ** -0.5, 0.15625, ((2, 32),))
    right_factors = normal_values(streams_of[1], (NAUX, NB, V), NAUX ** -0.5, 0.15625)
    amplitudes = normal_values(streams_of[2], (NPAIR, V, V), (40.0 / V), 0.46875, ((1, 32),))
    return dict(left_factors=left_factors, right_factors=right_factors, amplitudes=amplitudes)


def reference(left_factors, right_factors, amplitudes):
    left_wide = left_factors.astype(jnp.float32)
    right_wide = right_factors.astype(jnp.float32)
    integrals = jnp.einsum('qac,qbd->cdab', left_wide, right_wide).astype(jnp.bfloat16)
    matrix = integrals.reshape(V * V, NA * NB)
    flat_amps = amplitudes.reshape(NPAIR, V * V)
    ladder = jnp.dot(flat_amps, matrix, preferred_element_type=jnp.float32)
    return ladder.reshape(NPAIR, NA, NB)
```

```python
import functools

import jax
import jax.numpy as jnp
from jax import lax
from jax.experimental import pallas as pl
from jax.experimental.pallas import tpu as pltpu
from jax.sharding import PartitionSpec as P

MESH = pl.DeviceIdType.MESH
LANES = 128


def ladder_kernel(
    n, fold, left_hbm, right_hbm, amps_hbm, out_ref,
    left_in, amps_in, right_in, left_f32, amps_f32, left_rows, amps_rows, right_cols,
    integrals, send_buf, recv_buf, load_sem, send_sem, recv_sem,
):
    count_a, c_block, naux = left_hbm.shape
    _, count_b, width = right_hbm.shape
    pairs = amps_hbm.shape[0]
    chunks = width // LANES
    own_a = count_a // n
    me = lax.axis_index("row")

    load_left = pltpu.make_async_copy(left_hbm, left_in, load_sem.at[0])
    load_amps = pltpu.make_async_copy(amps_hbm, amps_in, load_sem.at[1])
    load_right = [
        pltpu.make_async_copy(
            right_hbm.at[:, :, pl.ds(k * LANES, LANES)], right_in.at[k], load_sem.at[2 + k]
        )
        for k in range(chunks)
    ]
    load_left.start()
    for k in range(chunks // 2):
        load_right[k].start()
    load_amps.start()
    for k in range(chunks // 2, chunks):
        load_right[k].start()

    barrier = pltpu.get_barrier_semaphore()

    @pl.loop(1, n)
    def _(k):
        pl.semaphore_signal(
            barrier, inc=1, device_id={"row": lax.rem(me + k, n)}, device_id_type=MESH
        )

    load_left.wait()
    for k in range(naux // LANES):
        lanes = pl.ds(k * LANES, LANES)
        left_f32[k % 2] = left_in[:, :, lanes].astype(jnp.float32).reshape(count_a * c_block, LANES)
        for c in range(c_block):
            left_rows[pl.ds(c * count_a, count_a), lanes] = left_f32[
                k % 2, pl.ds(c, count_a, stride=c_block), :
            ].astype(jnp.bfloat16)

    rows = 256
    q_rows = rows // count_b
    i = lax.broadcasted_iota(jnp.int32, (rows, rows), 0)
    j = lax.broadcasted_iota(jnp.int32, (rows, rows), 1)
    pick = (j == (i % q_rows) * count_b + i // q_rows).astype(jnp.bfloat16)

    half = 2 * LANES
    total = None
    for h in range(width // half):
        load_right[2 * h].wait()
        load_right[2 * h + 1].wait()
        for s in range(naux // q_rows):
            part = jnp.concatenate(
                [
                    right_in[2 * h + e, pl.ds(s * q_rows, q_rows)].reshape(rows, LANES)
                    for e in range(2)
                ],
                axis=1,
            )
            moved = jnp.dot(pick, part, preferred_element_type=jnp.float32).astype(jnp.bfloat16)
            for b in range(count_b):
                right_cols[h % 2, pl.ds(s * q_rows, q_rows), pl.ds(b * half, half)] = moved[
                    b * q_rows : (b + 1) * q_rows
                ]
        for b in range(count_b):
            cols = pl.ds(b * half, half)
            integrals[h % 2, :, cols] = jnp.dot(
                left_rows[...], right_cols[h % 2, :, cols], preferred_element_type=jnp.float32
            ).astype(jnp.bfloat16)
        if h == 0:
            load_amps.wait()
            for k in range(chunks):
                lanes = pl.ds(k * LANES, LANES)
                amps_f32[k % 2] = amps_in[:, :, lanes].astype(jnp.float32).reshape(
                    pairs * c_block, LANES
                )
                for c in range(c_block):
                    picked = amps_f32[k % 2, pl.ds(c, pairs, stride=c_block), :].astype(jnp.bfloat16)
                    for f in range(fold):
                        amps_rows[c, pl.ds(f * pairs, pairs), lanes] = picked
        for c in range(c_block):
            block = jnp.concatenate(
                [
                    integrals[h % 2, pl.ds(c * count_a, count_a), pl.ds(b * half, half)]
                    for b in range(count_b)
                ],
                axis=0,
            )
            term = lax.dot_general(
                block, amps_rows[c, :, pl.ds(h * half, half)], (((1,), (1,)), ((), ())),
                preferred_element_type=jnp.float32,
            )
            total = term if total is None else total + term

    lane = lax.broadcasted_iota(jnp.int32, (count_a, fold * pairs), 1)
    for g in range(count_b // fold):
        row = total[g * fold * count_a : (g * fold + 1) * count_a]
        for f in range(1, fold):
            b = g * fold + f
            row = jnp.where(lane >= f * pairs, total[b * count_a : (b + 1) * count_a], row)
        send_buf[:, g, :] = row

    pl.semaphore_wait(barrier, n - 1)

    @pl.loop(1, n)
    def _(k):
        to = lax.rem(me + k, n)
        pltpu.make_async_remote_copy(
            src_ref=send_buf.at[pl.ds(to * own_a, own_a)],
            dst_ref=recv_buf.at[pl.ds((k - 1) * own_a, own_a)],
            send_sem=send_sem,
            recv_sem=recv_sem,
            device_id={"row": to},
            device_id_type=MESH,
        ).start()

    every = recv_buf.at[pl.ds(0, (n - 1) * own_a)]
    pltpu.make_async_copy(every, every, recv_sem).wait()
    mine = send_buf[pl.ds(me * own_a, own_a)]
    got = recv_buf[...].reshape((n - 1, own_a) + recv_buf.shape[1:])
    result = mine + jnp.sum(got, axis=0)
    for b in range(count_b):
        out_ref[:, b, :] = result[:, b // fold, (b % fold) * pairs : (b % fold + 1) * pairs]
    pltpu.make_async_copy(every, every, send_sem).wait()


def per_device(n, left_factors, right_factors, amplitudes):
    left = lax.all_gather(left_factors, "col", axis=0, tiled=True)
    right = lax.all_gather(right_factors, "col", axis=0, tiled=True)
    naux, count_a, c_block = left.shape
    _, count_b, width = right.shape
    pairs = amplitudes.shape[0]
    fold = 2 if 2 * pairs == LANES and count_b % 2 == 0 else 1
    own_a = count_a // n
    half = 2 * LANES
    anywhere = pl.BlockSpec(memory_space=pl.ANY)
    bf16, f32 = jnp.bfloat16, jnp.float32
    piece = (count_b // fold, fold * pairs)
    out = pl.pallas_call(
        functools.partial(ladder_kernel, n, fold),
        out_shape=jax.ShapeDtypeStruct((own_a, count_b, pairs), f32),
        in_specs=[anywhere] * 3,
        out_specs=pl.BlockSpec(memory_space=pltpu.VMEM),
        scratch_shapes=[
            pltpu.VMEM((count_a, c_block, naux), bf16),
            pltpu.VMEM((pairs, c_block, width), bf16),
            pltpu.VMEM((width // LANES, naux, count_b, LANES), bf16),
            pltpu.VMEM((2, count_a * c_block, LANES), f32),
            pltpu.VMEM((2, pairs * c_block, LANES), f32),
            pltpu.VMEM((c_block * count_a, naux), bf16),
            pltpu.VMEM((c_block, fold * pairs, width), bf16),
            pltpu.VMEM((2, naux, count_b * half), bf16),
            pltpu.VMEM((2, c_block * count_a, count_b * half), bf16),
            pltpu.VMEM((count_a,) + piece, f32),
            pltpu.VMEM(((n - 1) * own_a,) + piece, f32),
            pltpu.SemaphoreType.DMA((2 + width // LANES,)),
            pltpu.SemaphoreType.DMA,
            pltpu.SemaphoreType.DMA,
        ],
        compiler_params=pltpu.CompilerParams(
            collective_id=0, has_side_effects=True, vmem_limit_bytes=48 * 1024 * 1024
        ),
        name="ladder",
    )(jnp.transpose(left, (1, 2, 0)), right, amplitudes)
    return jnp.transpose(out, (2, 0, 1))


def solution(mesh):
    placed = (P("col", None, "row"), P("col", None, None), P("col", "row", None))
    return jax.shard_map(
        functools.partial(per_device, mesh.shape["row"]),
        mesh=mesh, in_specs=placed, out_specs=P("col", "row", None), check_vma=False,
    )
```

```python
import functools

import jax
import jax.numpy as jnp
from jax import lax
from jax.experimental import pallas as pl
from jax.experimental.pallas import tpu as pltpu
from jax.sharding import PartitionSpec as P

MESH = pl.DeviceIdType.MESH
LANES = 128


def ladder_kernel(
    n, fold, left_hbm, right_hbm, amps_hbm, out_ref,
    left_in, amps_in, right_in, left_f32, left_rows, amps_f32, amps_rows, right_f32, right_cols,
    integrals, send_buf, recv_buf, load_sem, send_sem, recv_sem,
):
    count_a, c_block, naux = left_hbm.shape
    _, count_b, width = right_hbm.shape
    pairs = amps_hbm.shape[0]
    chunks = width // LANES
    own_a = count_a // n
    deep = 2 if c_block % 2 == 0 else 1
    me = lax.axis_index("row")

    load_left = pltpu.make_async_copy(left_hbm, left_in, load_sem.at[0])
    load_amps = pltpu.make_async_copy(amps_hbm, amps_in, load_sem.at[1])
    load_right = [
        pltpu.make_async_copy(
            right_hbm.at[:, :, pl.ds(k * LANES, LANES)], right_in.at[k], load_sem.at[2 + k]
        )
        for k in range(chunks)
    ]
    load_left.start()
    for k in range(chunks // 2):
        load_right[k].start()
    load_amps.start()
    for k in range(chunks // 2, chunks):
        load_right[k].start()

    barrier = pltpu.get_barrier_semaphore()

    @pl.loop(1, n)
    def _(k):
        pl.semaphore_signal(
            barrier, inc=1, device_id={"row": lax.rem(me + k, n)}, device_id_type=MESH
        )

    load_left.wait()
    for k in range(naux // LANES):
        lanes = pl.ds(k * LANES, LANES)
        left_f32[k % 2] = left_in[:, :, lanes].astype(jnp.float32).reshape(count_a * c_block, LANES)
        for c in range(c_block):
            left_rows[pl.ds(c * count_a, count_a), lanes] = left_f32[
                k % 2, pl.ds(c, count_a, stride=c_block), :
            ].astype(jnp.bfloat16)

    def split_right(k):
        staged, columns = right_f32[k % 2], right_cols[k % 2]
        flat = right_in.at[k].reshape(naux * count_b, LANES)
        step = 64
        for s in range(naux // step):
            rows = pl.ds(s * step * count_b, step * count_b)
            staged[rows, :] = flat[rows, :].astype(jnp.float32)
            for b in range(count_b):
                columns[pl.ds(s * step, step), pl.ds(b * LANES, LANES)] = staged[
                    pl.ds(s * step * count_b + b, step, stride=count_b), :
                ].astype(jnp.bfloat16)

    def split_amps(k):
        lanes = pl.ds(k * LANES, LANES)
        staged = amps_f32[k % 2]
        staged[...] = amps_in[:, :, lanes].astype(jnp.float32).reshape(pairs * c_block, LANES)
        for c in range(c_block):
            picked = staged[pl.ds(c, pairs, stride=c_block), :].astype(jnp.bfloat16)
            for f in range(fold):
                amps_rows[k % 2][
                    c // deep, pl.ds(f * pairs, pairs), pl.ds((c % deep) * LANES, LANES)
                ] = picked

    def integrate(k):
        for b in range(0, count_b, 2):
            cols = pl.ds(b * LANES, min(2, count_b - b) * LANES)
            integrals[k % 2][:, cols] = jnp.dot(
                left_rows[...], right_cols[k % 2][:, cols], preferred_element_type=jnp.float32
            ).astype(jnp.bfloat16)

    def contract(k, total):
        for g in range(c_block // deep):
            block = jnp.concatenate(
                [
                    jnp.concatenate(
                        [
                            integrals[k % 2][
                                pl.ds((g * deep + e) * count_a, count_a), pl.ds(b * LANES, LANES)
                            ]
                            for e in range(deep)
                        ],
                        axis=1,
                    )
                    for b in range(count_b)
                ],
                axis=0,
            )
            term = lax.dot_general(
                block, amps_rows[k % 2][g], (((1,), (1,)), ((), ())),
                preferred_element_type=jnp.float32,
            )
            total = term if total is None else total + term
        return total

    load_right[0].wait()
    split_right(0)
    total = None
    for k in range(chunks):
        if k + 1 < chunks:
            load_right[k + 1].wait()
        if k == 0:
            load_amps.wait()
        integrate(k)
        if k + 1 < chunks:
            split_right(k + 1)
        if k > 0:
            total = contract(k - 1, total)
        split_amps(k)
    total = contract(chunks - 1, total)

    lane = lax.broadcasted_iota(jnp.int32, (count_a, fold * pairs), 1)
    for g in range(count_b // fold):
        row = total[g * fold * count_a : (g * fold + 1) * count_a]
        for f in range(1, fold):
            b = g * fold + f
            row = jnp.where(lane >= f * pairs, total[b * count_a : (b + 1) * count_a], row)
        send_buf[:, g, :] = row

    pl.semaphore_wait(barrier, n - 1)

    @pl.loop(1, n)
    def _(k):
        to = lax.rem(me + k, n)
        pltpu.make_async_remote_copy(
            src_ref=send_buf.at[pl.ds(to * own_a, own_a)],
            dst_ref=recv_buf.at[pl.ds((k - 1) * own_a, own_a)],
            send_sem=send_sem,
            recv_sem=recv_sem,
            device_id={"row": to},
            device_id_type=MESH,
        ).start()

    every = recv_buf.at[pl.ds(0, (n - 1) * own_a)]
    pltpu.make_async_copy(every, every, recv_sem).wait()
    mine = send_buf[pl.ds(me * own_a, own_a)]
    got = recv_buf[...].reshape((n - 1, own_a) + recv_buf.shape[1:])
    result = mine + jnp.sum(got, axis=0)
    for b in range(count_b):
        out_ref[:, b, :] = result[:, b // fold, (b % fold) * pairs : (b % fold + 1) * pairs]
    pltpu.make_async_copy(every, every, send_sem).wait()


def per_device(n, left_factors, right_factors, amplitudes):
    left = lax.all_gather(left_factors, "col", axis=0, tiled=True)
    right = lax.all_gather(right_factors, "col", axis=0, tiled=True)
    naux, count_a, c_block = left.shape
    _, count_b, width = right.shape
    pairs = amplitudes.shape[0]
    fold = 2 if 2 * pairs == LANES and count_b % 2 == 0 else 1
    own_a = count_a // n
    deep = 2 if c_block % 2 == 0 else 1
    anywhere = pl.BlockSpec(memory_space=pl.ANY)
    bf16, f32 = jnp.bfloat16, jnp.float32
    piece = (count_b // fold, fold * pairs)
    out = pl.pallas_call(
        functools.partial(ladder_kernel, n, fold),
        out_shape=jax.ShapeDtypeStruct((own_a, count_b, pairs), f32),
        in_specs=[anywhere] * 3,
        out_specs=pl.BlockSpec(memory_space=pltpu.VMEM),
        scratch_shapes=[
            pltpu.VMEM((count_a, c_block, naux), bf16),
            pltpu.VMEM((pairs, c_block, width), bf16),
            pltpu.VMEM((width // LANES, naux, count_b, LANES), bf16),
            pltpu.VMEM((2, count_a * c_block, LANES), f32),
            pltpu.VMEM((c_block * count_a, naux), bf16),
            [pltpu.VMEM((pairs * c_block, LANES), f32)] * 2,
            [pltpu.VMEM((c_block // deep, fold * pairs, deep * LANES), bf16)] * 2,
            [pltpu.VMEM((naux * count_b, LANES), f32)] * 2,
            [pltpu.VMEM((naux, count_b * LANES), bf16)] * 2,
            [pltpu.VMEM((c_block * count_a, count_b * LANES), bf16)] * 2,
            pltpu.VMEM((count_a,) + piece, f32),
            pltpu.VMEM(((n - 1) * own_a,) + piece, f32),
            pltpu.SemaphoreType.DMA((2 + width // LANES,)),
            pltpu.SemaphoreType.DMA,
            pltpu.SemaphoreType.DMA,
        ],
        compiler_params=pltpu.CompilerParams(
            collective_id=0, has_side_effects=True, vmem_limit_bytes=62 * 1024 * 1024
        ),
        name="ladder",
    )(jnp.transpose(left, (1, 2, 0)), right, amplitudes)
    return jnp.transpose(out, (2, 0, 1))


def solution(mesh):
    placed = (P("col", None, "row"), P("col", None, None), P("col", "row", None))
    return jax.shard_map(
        functools.partial(per_device, mesh.shape["row"]),
        mesh=mesh, in_specs=placed, out_specs=P("col", "row", None), check_vma=False,
    )
```

```python
import functools

import jax
import jax.numpy as jnp
from jax import lax
from jax.experimental import pallas as pl
from jax.experimental.pallas import tpu as pltpu
from jax.sharding import PartitionSpec as P

MESH = pl.DeviceIdType.MESH
LANES = 128


def ladder_kernel(
    n, fold, left_hbm, right_hbm, amps_hbm, out_ref,
    left_in, amps_in, right_in, left_f32, left_rows, amps_f32, amps_rows, right_f32, right_cols,
    integrals, send_buf, recv_buf, load_sem, send_sem, recv_sem,
):
    count_a, c_block, naux = left_hbm.shape
    _, count_b, width = right_hbm.shape
    pairs = amps_hbm.shape[0]
    chunks = width // LANES
    own_a = count_a // n
    deep = 2 if c_block % 2 == 0 else 1
    me = lax.axis_index("row")

    load_left = pltpu.make_async_copy(left_hbm, left_in, load_sem.at[0])
    load_amps = pltpu.make_async_copy(amps_hbm, amps_in, load_sem.at[1])

    def load_right(k):
        lanes = pl.ds(pl.multiple_of(k * LANES, LANES), LANES)
        return pltpu.make_async_copy(
            right_hbm.at[:, :, lanes], right_in.at[k], load_sem.at[2 + k]
        )

    load_left.start()
    for k in range(chunks // 2):
        load_right(k).start()
    load_amps.start()
    for k in range(chunks // 2, chunks):
        load_right(k).start()

    barrier = pltpu.get_barrier_semaphore()

    @pl.loop(1, n)
    def _(k):
        pl.semaphore_signal(
            barrier, inc=1, device_id={"row": lax.rem(me + k, n)}, device_id_type=MESH
        )

    load_left.wait()
    left_lanes = naux // LANES
    turn = 2 if left_lanes % 2 == 0 else 1

    @pl.loop(0, left_lanes // turn)
    def _(t):
        for e in range(turn):
            lanes = pl.ds(pl.multiple_of((t * turn + e) * LANES, LANES), LANES)
            staged = left_f32[e]
            staged[...] = left_in[:, :, lanes].astype(jnp.float32).reshape(count_a * c_block, LANES)
            for c in range(c_block):
                left_rows[pl.ds(c * count_a, count_a), lanes] = staged[
                    pl.ds(c, count_a, stride=c_block), :
                ].astype(jnp.bfloat16)

    def split_right(k, slot):
        staged, columns = right_f32[slot], right_cols[slot]
        flat = right_in.at[k].reshape(naux * count_b, LANES)
        step = 64
        for s in range(naux // step):
            rows = pl.ds(s * step * count_b, step * count_b)
            staged[rows, :] = flat[rows, :].astype(jnp.float32)
            for b in range(count_b):
                columns[pl.ds(s * step, step), pl.ds(b * LANES, LANES)] = staged[
                    pl.ds(s * step * count_b + b, step, stride=count_b), :
                ].astype(jnp.bfloat16)

    def split_amps(k, slot):
        lanes = pl.ds(pl.multiple_of(k * LANES, LANES), LANES)
        staged = amps_f32[slot]
        staged[...] = amps_in[:, :, lanes].astype(jnp.float32).reshape(pairs * c_block, LANES)
        for c in range(c_block):
            picked = staged[pl.ds(c, pairs, stride=c_block), :].astype(jnp.bfloat16)
            for f in range(fold):
                amps_rows[slot][
                    c // deep, pl.ds(f * pairs, pairs), pl.ds((c % deep) * LANES, LANES)
                ] = picked

    def integrate(slot):
        for b in range(0, count_b, 2):
            cols = pl.ds(b * LANES, min(2, count_b - b) * LANES)
            integrals[slot][:, cols] = jnp.dot(
                left_rows[...], right_cols[slot][:, cols], preferred_element_type=jnp.float32
            ).astype(jnp.bfloat16)

    def contract(slot):
        total = None
        for g in range(c_block // deep):
            block = jnp.concatenate(
                [
                    jnp.concatenate(
                        [
                            integrals[slot][
                                pl.ds((g * deep + e) * count_a, count_a), pl.ds(b * LANES, LANES)
                            ]
                            for e in range(deep)
                        ],
                        axis=1,
                    )
                    for b in range(count_b)
                ],
                axis=0,
            )
            term = lax.dot_general(
                block, amps_rows[slot][g], (((1,), (1,)), ((), ())),
                preferred_element_type=jnp.float32,
            )
            total = term if total is None else total + term
        return total

    load_right(0).wait()
    split_right(0, 0)
    integrals[1][...] = jnp.zeros_like(integrals[1])
    amps_rows[1][...] = jnp.zeros_like(amps_rows[1])
    load_amps.wait()

    def step(k, slot, total):
        @pl.when(k + 1 < chunks)
        def _():
            load_right(k + 1).wait()

        integrate(slot)
        split_right(lax.rem(k + 1, chunks), 1 - slot)
        total = total + contract(1 - slot)
        split_amps(k, slot)
        return total

    total = lax.fori_loop(
        0, chunks // 2, lambda t, total: step(2 * t + 1, 1, step(2 * t, 0, total)),
        jnp.zeros((count_b * count_a, fold * pairs), jnp.float32),
    )
    total = total + contract(1)

    lane = lax.broadcasted_iota(jnp.int32, (count_a, fold * pairs), 1)
    for g in range(count_b // fold):
        row = total[g * fold * count_a : (g * fold + 1) * count_a]
        for f in range(1, fold):
            b = g * fold + f
            row = jnp.where(lane >= f * pairs, total[b * count_a : (b + 1) * count_a], row)
        send_buf[:, g, :] = row

    pl.semaphore_wait(barrier, n - 1)

    @pl.loop(1, n)
    def _(k):
        to = lax.rem(me + k, n)
        pltpu.make_async_remote_copy(
            src_ref=send_buf.at[pl.ds(to * own_a, own_a)],
            dst_ref=recv_buf.at[pl.ds((k - 1) * own_a, own_a)],
            send_sem=send_sem,
            recv_sem=recv_sem,
            device_id={"row": to},
            device_id_type=MESH,
        ).start()

    every = recv_buf.at[pl.ds(0, (n - 1) * own_a)]
    pltpu.make_async_copy(every, every, recv_sem).wait()
    mine = send_buf[pl.ds(me * own_a, own_a)]
    got = recv_buf[...].reshape((n - 1, own_a) + recv_buf.shape[1:])
    result = mine + jnp.sum(got, axis=0)
    for b in range(count_b):
        out_ref[:, b, :] = result[:, b // fold, (b % fold) * pairs : (b % fold + 1) * pairs]
    pltpu.make_async_copy(every, every, send_sem).wait()


def per_device(n, left_factors, right_factors, amplitudes):
    left = lax.all_gather(left_factors, "col", axis=0, tiled=True)
    right = lax.all_gather(right_factors, "col", axis=0, tiled=True)
    naux, count_a, c_block = left.shape
    _, count_b, width = right.shape
    pairs = amplitudes.shape[0]
    fold = 2 if 2 * pairs == LANES and count_b % 2 == 0 else 1
    own_a = count_a // n
    deep = 2 if c_block % 2 == 0 else 1
    anywhere = pl.BlockSpec(memory_space=pl.ANY)
    bf16, f32 = jnp.bfloat16, jnp.float32
    piece = (count_b // fold, fold * pairs)
    out = pl.pallas_call(
        functools.partial(ladder_kernel, n, fold),
        out_shape=jax.ShapeDtypeStruct((own_a, count_b, pairs), f32),
        in_specs=[anywhere] * 3,
        out_specs=pl.BlockSpec(memory_space=pltpu.VMEM),
        scratch_shapes=[
            pltpu.VMEM((count_a, c_block, naux), bf16),
            pltpu.VMEM((pairs, c_block, width), bf16),
            pltpu.VMEM((width // LANES, naux, count_b, LANES), bf16),
            [pltpu.VMEM((count_a * c_block, LANES), f32)] * 2,
            pltpu.VMEM((c_block * count_a, naux), bf16),
            [pltpu.VMEM((pairs * c_block, LANES), f32)] * 2,
            [pltpu.VMEM((c_block // deep, fold * pairs, deep * LANES), bf16)] * 2,
            [pltpu.VMEM((naux * count_b, LANES), f32)] * 2,
            [pltpu.VMEM((naux, count_b * LANES), bf16)] * 2,
            [pltpu.VMEM((c_block * count_a, count_b * LANES), bf16)] * 2,
            pltpu.VMEM((count_a,) + piece, f32),
            pltpu.VMEM(((n - 1) * own_a,) + piece, f32),
            pltpu.SemaphoreType.DMA((2 + width // LANES,)),
            pltpu.SemaphoreType.DMA,
            pltpu.SemaphoreType.DMA,
        ],
        compiler_params=pltpu.CompilerParams(
            collective_id=0, has_side_effects=True, vmem_limit_bytes=53 * 1024 * 1024
        ),
        name="ladder",
    )(jnp.transpose(left, (1, 2, 0)), right, amplitudes)
    return jnp.transpose(out, (2, 0, 1))


def solution(mesh):
    placed = (P("col", None, "row"), P("col", None, None), P("col", "row", None))
    return jax.shard_map(
        functools.partial(per_device, mesh.shape["row"]),
        mesh=mesh, in_specs=placed, out_specs=P("col", "row", None), check_vma=False,
    )
```

```python
import functools

import jax
import jax.numpy as jnp
from jax import lax
from jax.experimental import pallas as pl
from jax.experimental.pallas import tpu as pltpu
from jax.sharding import PartitionSpec as P

MESH = pl.DeviceIdType.MESH
LANES = 128
TILE = 256
LEFT_PIECES = 3


def ladder_kernel(
    n, fold, left_hbm, right_hbm, amps_hbm, out_ref,
    left_in, amps_in, right_in, left_f32, left_rows, amps_f32, amps_rows, right_f32, right_cols,
    integrals, total_buf, send_buf, recv_buf, load_sem, send_sem, recv_sem,
):
    count_a, c_block, naux = left_hbm.shape
    _, count_b, width = right_hbm.shape
    pairs = amps_hbm.shape[0]
    chunks = width // LANES
    own_a = count_a // n
    me = lax.axis_index("row")

    left_lanes = naux // LANES
    q_tiles = naux // TILE
    m_halves = count_a * c_block // TILE

    def load_left(p):
        lanes = pl.ds(p * (naux // LEFT_PIECES), naux // LEFT_PIECES)
        return pltpu.make_async_copy(
            left_hbm.at[:, :, lanes], left_in.at[:, :, lanes], load_sem.at[1 + chunks + p]
        )

    load_amps = pltpu.make_async_copy(amps_hbm, amps_in, load_sem.at[0])

    def load_right(k):
        lanes = pl.ds(pl.multiple_of(k * LANES, LANES), LANES)
        return pltpu.make_async_copy(
            right_hbm.at[:, :, lanes], right_in.at[k], load_sem.at[1 + k]
        )

    for p in range(LEFT_PIECES):
        load_left(p).start()
    for k in range(chunks // 2):
        load_right(k).start()
    load_amps.start()
    for k in range(chunks // 2, chunks):
        load_right(k).start()

    barrier = pltpu.get_barrier_semaphore()

    @pl.loop(1, n)
    def _(k):
        pl.semaphore_signal(
            barrier, inc=1, device_id={"row": lax.rem(me + k, n)}, device_id_type=MESH
        )

    turn = 2
    for p in range(LEFT_PIECES):
        load_left(p).wait()

        @pl.loop(0, left_lanes // (LEFT_PIECES * turn))
        def _(t):
            for e in range(turn):
                at = p * (left_lanes // LEFT_PIECES) + t * turn + e
                lanes = pl.ds(pl.multiple_of(at * LANES, LANES), LANES)
                staged = left_f32[e]
                staged[...] = (
                    left_in[:, :, lanes].astype(jnp.float32).reshape(count_a * c_block, LANES)
                )
                for c in range(c_block):
                    left_rows[pl.ds(c * count_a, count_a), lanes] = staged[
                        pl.ds(c, count_a, stride=c_block), :
                    ].astype(jnp.bfloat16)

    def split_right(k, kt):
        staged, columns = right_f32[k % 2], right_cols[k % 2]
        flat = right_in.at[k].reshape(naux * count_b, LANES)
        step = 64
        for s in range(kt * TILE // step, (kt + 1) * TILE // step):
            rows = pl.ds(s * step * count_b, step * count_b)
            staged[rows, :] = flat[rows, :].astype(jnp.float32)
            for b in range(count_b):
                columns[pl.ds(s * step, step), pl.ds(b * LANES, LANES)] = staged[
                    pl.ds(s * step * count_b + b, step, stride=count_b), :
                ].astype(jnp.bfloat16)

    def split_amps(k, kt):
        lanes = pl.ds(k * LANES, LANES)
        staged = amps_f32[k % 2]
        if kt == 0:
            staged[...] = amps_in[:, :, lanes].astype(jnp.float32).reshape(pairs * c_block, LANES)
        for c in range(kt * c_block // q_tiles, (kt + 1) * c_block // q_tiles):
            picked = staged[pl.ds(c, pairs, stride=c_block), :].astype(jnp.bfloat16)
            for f in range(fold):
                amps_rows[k % 2][
                    pl.ds(((c // 2) * fold + f) * pairs, pairs), pl.ds((c % 2) * LANES, LANES)
                ] = picked

    def block_of(k, g):
        return jnp.concatenate(
            [
                jnp.concatenate(
                    [
                        integrals[k % 2][
                            pl.ds((g * 2 + e) * count_a, count_a), pl.ds(b * LANES, LANES)
                        ]
                        for e in range(2)
                    ],
                    axis=1,
                )
                for b in range(count_b)
            ],
            axis=0,
        )

    def integrate(acc, k, kt):
        def push(m, staging):
            pltpu.matmul_push_rhs(
                right_cols[k % 2][pl.ds(kt * TILE, TILE), pl.ds(m * TILE, TILE)], staging, m
            )

        def multiply(m, staging):
            for h in range(m_halves):
                pltpu.matmul_acc_lhs(
                    acc[m][h], left_rows[pl.ds(h * TILE, TILE), pl.ds(kt * TILE, TILE)],
                    load_staged_rhs=staging if h == 0 else None,
                )

        def finish():
            if kt == q_tiles - 1:
                for h in range(m_halves):
                    for m in range(2):
                        integrals[k % 2][pl.ds(h * TILE, TILE), pl.ds(m * TILE, TILE)] = (
                            pltpu.matmul_pop(acc[m][h]).astype(jnp.bfloat16)
                        )

        return push, multiply, finish

    def contract(acc_out, k, p):
        def push(m, staging):
            pltpu.matmul_push_rhs(
                amps_rows[k % 2][pl.ds((2 * p + m) * TILE, TILE), :], staging, m, transpose=True
            )

        def multiply(m, staging):
            for e in range(2):
                pltpu.matmul_acc_lhs(
                    acc_out[m][e], block_of(k, 2 * (2 * p + m) + e),
                    load_staged_rhs=staging if e == 0 else None,
                )

        return push, multiply, lambda: None

    def arrived(k):
        if k + 1 < chunks:
            load_right(k + 1).wait()
        if k == 0:
            load_amps.wait()

    def on_units(acc, acc_out):
        tiles = []
        for k in range(chunks):
            for kt in range(q_tiles):
                beside = []
                if k + 1 < chunks:
                    beside.append(functools.partial(split_right, k + 1, kt))
                beside.append(functools.partial(split_amps, k, kt))
                before = functools.partial(arrived, k) if kt == 0 else None
                tiles.append((integrate(acc, k, kt), before, beside))
                if k > 0 and kt in (1, 2):
                    tiles.append((contract(acc_out, k - 1, kt - 1), None, []))
        tiles += [(contract(acc_out, chunks - 1, p), None, []) for p in range(2)]

        load_right(0).wait()
        for kt in range(q_tiles):
            split_right(0, kt)
        for m in range(2):
            tiles[0][0][0](m, 0)
        for i, ((_, multiply, finish), before, beside) in enumerate(tiles):
            if before is not None:
                before()
            if i + 1 < len(tiles):
                for m in range(2):
                    tiles[i + 1][0][0](m, (i + 1) % 2)
            for m in range(2):
                multiply(m, i % 2)
            for run in beside:
                run()
            finish()
        total = 0.0
        for m in range(2):
            for e in range(2):
                total += pltpu.matmul_pop(acc_out[m][e])[:, e * LANES : (e + 1) * LANES]
        total_buf[...] = total

    pl.run_scoped(
        on_units,
        [[pltpu.ACC(m)((TILE, TILE), jnp.float32)] * m_halves for m in range(2)],
        [[pltpu.ACC(m)((count_a * count_b, TILE), jnp.float32)] * 2 for m in range(2)],
    )
    total = total_buf[...]

    lane = lax.broadcasted_iota(jnp.int32, (count_a, fold * pairs), 1)
    for g in range(count_b // fold):
        row = total[g * fold * count_a : (g * fold + 1) * count_a]
        for f in range(1, fold):
            b = g * fold + f
            row = jnp.where(lane >= f * pairs, total[b * count_a : (b + 1) * count_a], row)
        send_buf[:, g, :] = row

    pl.semaphore_wait(barrier, n - 1)

    @pl.loop(1, n)
    def _(k):
        to = lax.rem(me + k, n)
        pltpu.make_async_remote_copy(
            src_ref=send_buf.at[pl.ds(to * own_a, own_a)],
            dst_ref=recv_buf.at[pl.ds((k - 1) * own_a, own_a)],
            send_sem=send_sem,
            recv_sem=recv_sem,
            device_id={"row": to},
            device_id_type=MESH,
        ).start()

    every = recv_buf.at[pl.ds(0, (n - 1) * own_a)]
    pltpu.make_async_copy(every, every, recv_sem).wait()
    mine = send_buf[pl.ds(me * own_a, own_a)]
    got = recv_buf[...].reshape((n - 1, own_a) + recv_buf.shape[1:])
    result = mine + jnp.sum(got, axis=0)
    for b in range(count_b):
        out_ref[:, b, :] = result[:, b // fold, (b % fold) * pairs : (b % fold + 1) * pairs]
    pltpu.make_async_copy(every, every, send_sem).wait()


def per_device(n, left_factors, right_factors, amplitudes):
    left = lax.all_gather(left_factors, "col", axis=0, tiled=True)
    right = lax.all_gather(right_factors, "col", axis=0, tiled=True)
    naux, count_a, c_block = left.shape
    _, count_b, width = right.shape
    pairs = amplitudes.shape[0]
    fold = 2 if 2 * pairs == LANES and count_b % 2 == 0 else 1
    own_a = count_a // n
    anywhere = pl.BlockSpec(memory_space=pl.ANY)
    bf16, f32 = jnp.bfloat16, jnp.float32
    piece = (count_b // fold, fold * pairs)
    out = pl.pallas_call(
        functools.partial(ladder_kernel, n, fold),
        out_shape=jax.ShapeDtypeStruct((own_a, count_b, pairs), f32),
        in_specs=[anywhere] * 3,
        out_specs=pl.BlockSpec(memory_space=pltpu.VMEM),
        scratch_shapes=[
            pltpu.VMEM((count_a, c_block, naux), bf16),
            pltpu.VMEM((pairs, c_block, width), bf16),
            pltpu.VMEM((width // LANES, naux, count_b, LANES), bf16),
            [pltpu.VMEM((count_a * c_block, LANES), f32)] * 2,
            pltpu.VMEM((c_block * count_a, naux), bf16),
            [pltpu.VMEM((pairs * c_block, LANES), f32)] * 2,
            [pltpu.VMEM((c_block // 2 * fold * pairs, TILE), bf16)] * 2,
            [pltpu.VMEM((naux * count_b, LANES), f32)] * 2,
            [pltpu.VMEM((naux, count_b * LANES), bf16)] * 2,
            [pltpu.VMEM((c_block * count_a, count_b * LANES), bf16)] * 2,
            pltpu.VMEM((count_b * count_a, fold * pairs), f32),
            pltpu.VMEM((count_a,) + piece, f32),
            pltpu.VMEM(((n - 1) * own_a,) + piece, f32),
            pltpu.SemaphoreType.DMA((1 + width // LANES + LEFT_PIECES,)),
            pltpu.SemaphoreType.DMA,
            pltpu.SemaphoreType.DMA,
        ],
        compiler_params=pltpu.CompilerParams(
            collective_id=0, has_side_effects=True, vmem_limit_bytes=53 * 1024 * 1024
        ),
        name="ladder",
    )(jnp.transpose(left, (1, 2, 0)), right, amplitudes)
    return jnp.transpose(out, (2, 0, 1))


def solution(mesh):
    placed = (P("col", None, "row"), P("col", None, None), P("col", "row", None))
    return jax.shard_map(
        functools.partial(per_device, mesh.shape["row"]),
        mesh=mesh, in_specs=placed, out_specs=P("col", "row", None), check_vma=False,
    )
```

```python
import functools

import jax
import jax.numpy as jnp
from jax import lax
from jax.experimental import pallas as pl
from jax.experimental.pallas import tpu as pltpu
from jax.sharding import PartitionSpec as P

MESH = pl.DeviceIdType.MESH
LANES = 128
TILE = 256


def ladder_kernel(
    n, fold, left_hbm, right_hbm, amps_hbm, out_ref,
    left_in, amps_in, right_in, left_f32, left_rows, amps_f32, amps_rows, right_f32,
    integrals, total_buf, send_buf, recv_buf, left_sem, right_sem, amps_sem, send_sem, recv_sem,
):
    count_a, c_block, naux = left_hbm.shape
    _, count_b, width = right_hbm.shape
    pairs = amps_hbm.shape[0]
    chunks = width // LANES
    own_a = count_a // n
    me = lax.axis_index("row")

    q_tiles = naux // TILE
    m_halves = count_a * c_block // TILE

    def load_left(kt):
        lanes = pl.ds(kt * TILE, TILE)
        return pltpu.make_async_copy(
            left_hbm.at[:, :, lanes], left_in.at[:, :, lanes], left_sem.at[kt]
        )

    def load_right(k, kt):
        rows = pl.ds(kt * TILE, TILE) if k == 0 else slice(None)
        return pltpu.make_async_copy(
            right_hbm.at[rows, :, pl.ds(k * LANES, LANES)], right_in.at[k, rows],
            right_sem.at[kt if k == 0 else q_tiles - 1 + k],
        )

    load_amps = pltpu.make_async_copy(amps_hbm, amps_in, amps_sem)
    for kt in range(q_tiles):
        load_left(kt).start()
        load_right(0, kt).start()
    for k in range(1, chunks):
        load_right(k, 0).start()
        if k == 1:
            load_amps.start()

    barrier = pltpu.get_barrier_semaphore()

    @pl.loop(1, n)
    def _(k):
        pl.semaphore_signal(
            barrier, inc=1, device_id={"row": lax.rem(me + k, n)}, device_id_type=MESH
        )

    def split_left(kt):
        load_left(kt).wait()
        for e in range(TILE // LANES):
            lanes = pl.ds(kt * TILE + e * LANES, LANES)
            staged = left_f32[e]
            staged[...] = (
                left_in[:, :, lanes].astype(jnp.float32).reshape(count_a * c_block, LANES)
            )
            for c in range(c_block):
                left_rows[pl.ds(c * count_a, count_a), lanes] = staged[
                    pl.ds(c, count_a, stride=c_block), :
                ].astype(jnp.bfloat16)

    def stage_right(i):
        k, kt = divmod(i, q_tiles)
        if k == 0 or kt == 0:
            load_right(k, kt).wait()
        flat = right_in.at[k].reshape(naux * count_b, LANES)
        right_f32[i % len(right_f32)][...] = flat[
            pl.ds(kt * TILE * count_b, TILE * count_b), :
        ].astype(jnp.float32)

    def split_amps(k, part, parts):
        lanes = pl.ds(k * LANES, LANES)
        staged = amps_f32[k % 2]
        if part == 0:
            if k == 0:
                load_amps.wait()
            staged[...] = amps_in[:, :, lanes].astype(jnp.float32).reshape(pairs * c_block, LANES)
        for c in range(part * c_block // parts, (part + 1) * c_block // parts):
            picked = staged[pl.ds(c, pairs, stride=c_block), :].astype(jnp.bfloat16)
            for f in range(fold):
                amps_rows[k % 2][
                    pl.ds(((c // 2) * fold + f) * pairs, pairs), pl.ds((c % 2) * LANES, LANES)
                ] = picked

    def block_of(k, g):
        return jnp.concatenate(
            [
                jnp.concatenate(
                    [
                        integrals[k % 2][
                            pl.ds((g * 2 + e) * count_a, count_a), pl.ds(b * LANES, LANES)
                        ]
                        for e in range(2)
                    ],
                    axis=1,
                )
                for b in range(count_b)
            ],
            axis=0,
        )

    def integrate(acc, k, kt):
        def push(m, staging):
            rows = right_f32[(k * q_tiles + kt) % len(right_f32)]
            tile = [
                rows[pl.ds(m * (count_b // 2) + e, TILE, stride=count_b), :].astype(jnp.bfloat16)
                for e in range(count_b // 2)
            ]
            pltpu.matmul_push_rhs(jnp.concatenate(tile, axis=1), staging, m)

        def multiply(m, staging):
            for h in range(m_halves):
                pltpu.matmul_acc_lhs(
                    acc[m][h], left_rows[pl.ds(h * TILE, TILE), pl.ds(kt * TILE, TILE)],
                    load_staged_rhs=staging if h == 0 else None,
                )

        def finish():
            if kt == q_tiles - 1:
                for h in range(m_halves):
                    for m in range(2):
                        integrals[k % 2][pl.ds(h * TILE, TILE), pl.ds(m * TILE, TILE)] = (
                            pltpu.matmul_pop(acc[m][h]).astype(jnp.bfloat16)
                        )

        return push, multiply, finish

    def contract(acc_out, k, p):
        def push(m, staging):
            pltpu.matmul_push_rhs(
                amps_rows[k % 2][pl.ds((2 * p + m) * TILE, TILE), :], staging, m, transpose=True
            )

        def multiply(m, staging):
            for e in range(2):
                pltpu.matmul_acc_lhs(
                    acc_out[m][e], block_of(k, 2 * (2 * p + m) + e),
                    load_staged_rhs=staging if e == 0 else None,
                )

        return push, multiply, lambda: None

    def on_units(acc, acc_out):
        tiles = []
        last = chunks * q_tiles
        half = q_tiles // 2
        for k in range(chunks):
            for kt in range(q_tiles):
                i = k * q_tiles + kt
                beside = []
                if i + 1 < q_tiles:
                    beside.append(functools.partial(split_left, i + 1))
                if i + 2 < last:
                    beside.append(functools.partial(stage_right, i + 2))
                if k > 0 and kt < half:
                    beside.append(functools.partial(split_amps, k - 1, kt, half))
                if k == chunks - 1 and kt >= half:
                    beside.append(functools.partial(split_amps, k, kt - half, q_tiles - half))
                tiles.append((integrate(acc, k, kt), beside))
                if k > 0 and kt in (half, half + 1):
                    tiles.append((contract(acc_out, k - 1, kt - half), []))
        tiles += [(contract(acc_out, chunks - 1, p), []) for p in range(2)]

        stage_right(0)
        split_left(0)
        stage_right(1)
        for m in range(2):
            tiles[0][0][0](m, 0)
        for i, ((_, multiply, finish), beside) in enumerate(tiles):
            if i + 1 < len(tiles):
                for m in range(2):
                    tiles[i + 1][0][0](m, (i + 1) % 2)
            for m in range(2):
                multiply(m, i % 2)
            for run in beside:
                run()
            finish()
        total = 0.0
        for m in range(2):
            for e in range(2):
                total += pltpu.matmul_pop(acc_out[m][e])[:, e * LANES : (e + 1) * LANES]
        total_buf[...] = total

    pl.run_scoped(
        on_units,
        [[pltpu.ACC(m)((TILE, TILE), jnp.float32)] * m_halves for m in range(2)],
        [[pltpu.ACC(m)((count_a * count_b, TILE), jnp.float32)] * 2 for m in range(2)],
    )
    total = total_buf[...]

    lane = lax.broadcasted_iota(jnp.int32, (count_a, fold * pairs), 1)
    for g in range(count_b // fold):
        row = total[g * fold * count_a : (g * fold + 1) * count_a]
        for f in range(1, fold):
            b = g * fold + f
            row = jnp.where(lane >= f * pairs, total[b * count_a : (b + 1) * count_a], row)
        send_buf[:, g, :] = row

    pl.semaphore_wait(barrier, n - 1)

    @pl.loop(1, n)
    def _(k):
        to = lax.rem(me + k, n)
        pltpu.make_async_remote_copy(
            src_ref=send_buf.at[pl.ds(to * own_a, own_a)],
            dst_ref=recv_buf.at[pl.ds((k - 1) * own_a, own_a)],
            send_sem=send_sem,
            recv_sem=recv_sem,
            device_id={"row": to},
            device_id_type=MESH,
        ).start()

    every = recv_buf.at[pl.ds(0, (n - 1) * own_a)]
    pltpu.make_async_copy(every, every, recv_sem).wait()
    mine = send_buf[pl.ds(me * own_a, own_a)]
    got = recv_buf[...].reshape((n - 1, own_a) + recv_buf.shape[1:])
    result = mine + jnp.sum(got, axis=0)
    for b in range(count_b):
        out_ref[:, b, :] = result[:, b // fold, (b % fold) * pairs : (b % fold + 1) * pairs]
    pltpu.make_async_copy(every, every, send_sem).wait()


def per_device(n, left_factors, right_factors, amplitudes):
    left = lax.all_gather(left_factors, "col", axis=0, tiled=True)
    right = lax.all_gather(right_factors, "col", axis=0, tiled=True)
    naux, count_a, c_block = left.shape
    _, count_b, width = right.shape
    pairs = amplitudes.shape[0]
    fold = 2 if 2 * pairs == LANES and count_b % 2 == 0 else 1
    own_a = count_a // n
    anywhere = pl.BlockSpec(memory_space=pl.ANY)
    bf16, f32 = jnp.bfloat16, jnp.float32
    piece = (count_b // fold, fold * pairs)
    out = pl.pallas_call(
        functools.partial(ladder_kernel, n, fold),
        out_shape=jax.ShapeDtypeStruct((own_a, count_b, pairs), f32),
        in_specs=[anywhere] * 3,
        out_specs=pl.BlockSpec(memory_space=pltpu.VMEM),
        scratch_shapes=[
            pltpu.VMEM((count_a, c_block, naux), bf16),
            pltpu.VMEM((pairs, c_block, width), bf16),
            pltpu.VMEM((width // LANES, naux, count_b, LANES), bf16),
            [pltpu.VMEM((count_a * c_block, LANES), f32)] * 2,
            pltpu.VMEM((c_block * count_a, naux), bf16),
            [pltpu.VMEM((pairs * c_block, LANES), f32)] * 2,
            [pltpu.VMEM((c_block // 2 * fold * pairs, TILE), bf16)] * 2,
            [pltpu.VMEM((TILE * count_b, LANES), f32)] * 4,
            [pltpu.VMEM((c_block * count_a, count_b * LANES), bf16)] * 2,
            pltpu.VMEM((count_b * count_a, fold * pairs), f32),
            pltpu.VMEM((count_a,) + piece, f32),
            pltpu.VMEM(((n - 1) * own_a,) + piece, f32),
            pltpu.SemaphoreType.DMA((naux // TILE,)),
            pltpu.SemaphoreType.DMA((naux // TILE + width // LANES - 1,)),
            pltpu.SemaphoreType.DMA,
            pltpu.SemaphoreType.DMA,
            pltpu.SemaphoreType.DMA,
        ],
        compiler_params=pltpu.CompilerParams(
            collective_id=0, has_side_effects=True, vmem_limit_bytes=53 * 1024 * 1024
        ),
        name="ladder",
    )(jnp.transpose(left, (1, 2, 0)), right, amplitudes)
    return jnp.transpose(out, (2, 0, 1))


def solution(mesh):
    placed = (P("col", None, "row"), P("col", None, None), P("col", "row", None))
    return jax.shard_map(
        functools.partial(per_device, mesh.shape["row"]),
        mesh=mesh, in_specs=placed, out_specs=P("col", "row", None), check_vma=False,
    )
```

```python
import functools

import jax
import jax.numpy as jnp
from jax import lax
from jax.experimental import pallas as pl
from jax.experimental.pallas import tpu as pltpu
from jax.sharding import PartitionSpec as P

MESH = pl.DeviceIdType.MESH
LANES = 128
TILE = 256


def ladder_kernel(
    n, fold, left_hbm, right_hbm, amps_hbm, out_ref,
    left_in, amps_in, right_in, picks, left_rows, amps_rows, right_cols,
    integrals, total_buf, send_buf, recv_buf, left_sem, right_sem, amps_sem, send_sem, recv_sem,
):
    count_a, c_block, naux = left_hbm.shape
    _, count_b, width = right_hbm.shape
    pairs = amps_hbm.shape[0]
    chunks = width // LANES
    own_a = count_a // n
    me = lax.axis_index("row")

    q_tiles = naux // TILE

    def load_left(kt):
        lanes = pl.ds(kt * TILE, TILE)
        return pltpu.make_async_copy(
            left_hbm.at[:, :, lanes], left_in.at[:, :, lanes], left_sem.at[kt]
        )

    def load_right(k, kt):
        early = k < 2
        rows = pl.ds(kt * TILE, TILE) if early else slice(None)
        return pltpu.make_async_copy(
            right_hbm.at[rows, :, pl.ds(k * LANES, LANES)], right_in.at[k, rows],
            right_sem.at[k * q_tiles + kt if early else 2 * q_tiles + k - 2],
        )

    load_amps = pltpu.make_async_copy(amps_hbm, amps_in, amps_sem)
    for kt in range(q_tiles):
        load_left(kt).start()
        for k in range(2):
            load_right(k, kt).start()
    for k in range(2, chunks):
        load_right(k, 0).start()
    load_amps.start()

    barrier = pltpu.get_barrier_semaphore()

    @pl.loop(1, n)
    def _(k):
        pl.semaphore_signal(
            barrier, inc=1, device_id={"row": lax.rem(me + k, n)}, device_id_type=MESH
        )

    i = lax.broadcasted_iota(jnp.int32, (TILE, TILE), 0)
    j = lax.broadcasted_iota(jnp.int32, (TILE, TILE), 1)
    q_rows = TILE // count_b
    outer = TILE // c_block
    picks[0] = (j == (i % q_rows) * count_b + i // q_rows).astype(jnp.bfloat16)
    picks[1] = (j == (i % outer) * c_block + i // outer).astype(jnp.bfloat16)

    def on_units(acc, moved):
        def move(which, slot, source, store, wait):
            def push(staging):
                wait()
                for m in range(2):
                    pltpu.matmul_push_rhs(source(m), staging, m)

            def multiply(staging):
                for m in range(2):
                    pltpu.matmul_acc_lhs(moved[m][slot], picks[which], load_staged_rhs=staging)

            def finish():
                for m in range(2):
                    store(m, pltpu.matmul_pop(moved[m][slot]).astype(jnp.bfloat16))

            return push, multiply, finish, ("moved", slot)

        def move_left(kt, slot):
            lanes = pl.ds(kt * TILE, TILE)

            def source(m):
                return left_in[pl.ds(m * outer, outer), :, lanes].reshape(TILE, TILE)

            def store(m, value):
                left_rows[pl.ds(m * TILE, TILE), lanes] = value

            return move(1, slot, source, store, lambda: load_left(kt).wait())

        def move_right(kk, kt, part, slot):
            def at(m):
                return kt * count_b + part * 2 + m

            def source(m):
                return jnp.concatenate(
                    [
                        right_in.at[2 * kk + e].reshape(naux * count_b, LANES)[
                            pl.ds(at(m) * TILE, TILE), :
                        ]
                        for e in range(2)
                    ],
                    axis=1,
                )

            def store(m, value):
                for b in range(count_b):
                    right_cols[kk][pl.ds(at(m) * q_rows, q_rows), pl.ds(b * TILE, TILE)] = value[
                        b * q_rows : (b + 1) * q_rows
                    ]

            def wait():
                if part == 0 and (kk == 0 or kt == 0):
                    for e in range(2):
                        load_right(2 * kk + e, kt).wait()

            return move(0, slot, source, store, wait)

        def move_amps(kk, part, slot):
            lanes = pl.ds(kk * TILE, TILE)

            def source(m):
                block = part * 2 + m
                return amps_in[pl.ds(block * outer, outer), :, lanes].reshape(TILE, TILE)

            def store(m, value):
                block = part * 2 + m
                for c in range(c_block):
                    amps_rows[kk][pl.ds(c * pairs + block * outer, outer), :] = value[
                        c * outer : (c + 1) * outer
                    ]

            def wait():
                if kk == 0 and part == 0:
                    load_amps.wait()

            return move(1, slot, source, store, wait)

        rows_of = count_a * c_block // len(acc[0])

        def integrate(kk, bb, kt):
            def push(staging):
                for m in range(2):
                    pltpu.matmul_push_rhs(
                        right_cols[kk][pl.ds(kt * TILE, TILE), pl.ds((2 * bb + m) * TILE, TILE)],
                        staging, m,
                    )

            def multiply(staging):
                for h in range(len(acc[0])):
                    for m in range(2):
                        pltpu.matmul_acc_lhs(
                            acc[m][h],
                            left_rows[pl.ds(h * rows_of, rows_of), pl.ds(kt * TILE, TILE)],
                            load_staged_rhs=staging if h == 0 else None,
                        )

            def finish():
                if kt == q_tiles - 1:
                    for h in range(len(acc[0])):
                        for m in range(2):
                            integrals[kk][
                                pl.ds(h * rows_of, rows_of), pl.ds((2 * bb + m) * TILE, TILE)
                            ] = pltpu.matmul_pop(acc[m][h]).astype(jnp.bfloat16)

            return push, multiply, finish, "acc" if kt == q_tiles - 1 else None

        def contract(kk, part):
            def group(m):
                return part * 2 + m

            def push(staging):
                for m in range(2):
                    pltpu.matmul_push_rhs(
                        amps_rows[kk][pl.ds(group(m) * TILE, TILE), :], staging, m, transpose=True
                    )

            def multiply(staging):
                for e in range(len(acc[0])):
                    for m in range(2):
                        c = group(m) * len(acc[0]) + e
                        block = [
                            integrals[kk][
                                pl.ds(h * TILE + c * outer, outer), pl.ds(b * TILE, TILE)
                            ]
                            for b in range(count_b)
                            for h in range(count_a // outer)
                        ]
                        pltpu.matmul_acc_lhs(
                            acc[m][e], jnp.concatenate(block, axis=0),
                            load_staged_rhs=staging if e == 0 else None,
                        )

            return push, multiply, lambda: None, None

        made = [0]

        def slot():
            made[0] += 1
            return made[0] % 2

        def moves(kt):
            return [move_left(kt, slot())] + [move_right(0, kt, p, slot()) for p in range(2)]

        tiles = moves(0) + moves(1)
        rest = [(kt, p) for kt in range(q_tiles) for p in range(2)]
        for kt in range(q_tiles):
            tiles.append(integrate(0, 0, kt))
            if kt + 2 < q_tiles:
                tiles += moves(kt + 2)
            else:
                tiles += [move_right(1, *rest.pop(0), slot()) for _ in range(2)]
        for kt in range(q_tiles):
            tiles.append(integrate(0, 1, kt))
            tiles += [move_right(1, *rest.pop(0), slot()) for _ in range(min(2, len(rest)))]
        later = [(kk, p) for kk in range(2) for p in range(2)]
        tiles.append(move_amps(*later.pop(0), slot()))
        for bb in range(2):
            for kt in range(q_tiles):
                tiles.append(integrate(1, bb, kt))
                if kt >= 3 and later:
                    tiles.append(move_amps(*later.pop(0), slot()))
        for kk in range(2):
            tiles += [contract(kk, p) for p in range(2)]

        pending = None
        tiles[0][0](0)
        for n_tile, (_, multiply, finish, key) in enumerate(tiles):
            if n_tile + 1 < len(tiles):
                tiles[n_tile + 1][0]((n_tile + 1) % 2)
            if pending is not None and pending[1] == "acc" and not isinstance(key, tuple):
                pending[0]()
                pending = None
            multiply(n_tile % 2)
            if pending is not None:
                pending[0]()
            pending = (finish, key)

        low, high = 0.0, 0.0
        for m in range(2):
            for e in range(len(acc[0])):
                lanes = e * pairs // LANES * LANES
                value = pltpu.matmul_pop(acc[m][e])[:, lanes : lanes + LANES]
                low, high = (low + value, high) if e % 2 == 0 else (low, high + value)
        lane = lax.broadcasted_iota(jnp.int32, low.shape, 1)
        both = jnp.where(lane < pairs, low, high)
        total_buf[...] = both + pltpu.roll(both, pairs, 1)

    pl.run_scoped(
        on_units,
        [
            [pltpu.ACC(m)((count_a * count_b, TILE), jnp.float32)] * (TILE // pairs)
            for m in range(2)
        ],
        [[pltpu.ACC(m)((TILE, TILE), jnp.float32)] * 2 for m in range(2)],
    )
    total = total_buf[...]

    lane = lax.broadcasted_iota(jnp.int32, (count_a, fold * pairs), 1)
    for g in range(count_b // fold):
        row = total[g * fold * count_a : (g * fold + 1) * count_a]
        for f in range(1, fold):
            b = g * fold + f
            row = jnp.where(lane >= f * pairs, total[b * count_a : (b + 1) * count_a], row)
        send_buf[:, g, :] = row

    pl.semaphore_wait(barrier, n - 1)

    @pl.loop(1, n)
    def _(k):
        to = lax.rem(me + k, n)
        pltpu.make_async_remote_copy(
            src_ref=send_buf.at[pl.ds(to * own_a, own_a)],
            dst_ref=recv_buf.at[pl.ds((k - 1) * own_a, own_a)],
            send_sem=send_sem,
            recv_sem=recv_sem,
            device_id={"row": to},
            device_id_type=MESH,
        ).start()

    every = recv_buf.at[pl.ds(0, (n - 1) * own_a)]
    pltpu.make_async_copy(every, every, recv_sem).wait()
    mine = send_buf[pl.ds(me * own_a, own_a)]
    got = recv_buf[...].reshape((n - 1, own_a) + recv_buf.shape[1:])
    result = mine + jnp.sum(got, axis=0)
    for b in range(count_b):
        out_ref[:, b, :] = result[:, b // fold, (b % fold) * pairs : (b % fold + 1) * pairs]
    pltpu.make_async_copy(every, every, send_sem).wait()


def per_device(n, left_factors, right_factors, amplitudes):
    left = lax.all_gather(left_factors, "col", axis=0, tiled=True)
    right = lax.all_gather(right_factors, "col", axis=0, tiled=True)
    naux, count_a, c_block = left.shape
    _, count_b, width = right.shape
    pairs = amplitudes.shape[0]
    fold = 2 if 2 * pairs == LANES and count_b % 2 == 0 else 1
    own_a = count_a // n
    anywhere = pl.BlockSpec(memory_space=pl.ANY)
    bf16, f32 = jnp.bfloat16, jnp.float32
    piece = (count_b // fold, fold * pairs)
    out = pl.pallas_call(
        functools.partial(ladder_kernel, n, fold),
        out_shape=jax.ShapeDtypeStruct((own_a, count_b, pairs), f32),
        in_specs=[anywhere] * 3,
        out_specs=pl.BlockSpec(memory_space=pltpu.VMEM),
        scratch_shapes=[
            pltpu.VMEM((count_a, c_block, naux), bf16),
            pltpu.VMEM((pairs, c_block, width), bf16),
            pltpu.VMEM((width // LANES, naux, count_b, LANES), bf16),
            pltpu.VMEM((2, TILE, TILE), bf16),
            pltpu.VMEM((c_block * count_a, naux), bf16),
            [pltpu.VMEM((c_block * pairs, TILE), bf16)] * (width // TILE),
            [pltpu.VMEM((naux, count_b * TILE), bf16)] * (width // TILE),
            [pltpu.VMEM((c_block * count_a, count_b * TILE), bf16)] * (width // TILE),
            pltpu.VMEM((count_b * count_a, fold * pairs), f32),
            pltpu.VMEM((count_a,) + piece, f32),
            pltpu.VMEM(((n - 1) * own_a,) + piece, f32),
            pltpu.SemaphoreType.DMA((naux // TILE,)),
            pltpu.SemaphoreType.DMA((2 * (naux // TILE) + width // LANES - 2,)),
            pltpu.SemaphoreType.DMA,
            pltpu.SemaphoreType.DMA,
            pltpu.SemaphoreType.DMA,
        ],
        compiler_params=pltpu.CompilerParams(
            collective_id=0, has_side_effects=True, vmem_limit_bytes=53 * 1024 * 1024
        ),
        name="ladder",
    )(jnp.transpose(left, (1, 2, 0)), right, amplitudes)
    return jnp.transpose(out, (2, 0, 1))


def solution(mesh):
    placed = (P("col", None, "row"), P("col", None, None), P("col", "row", None))
    return jax.shard_map(
        functools.partial(per_device, mesh.shape["row"]),
        mesh=mesh, in_specs=placed, out_specs=P("col", "row", None), check_vma=False,
    )
```

```python
import functools

import jax
import jax.numpy as jnp
from jax import lax
from jax.experimental import pallas as pl
from jax.experimental.pallas import tpu as pltpu
from jax.sharding import PartitionSpec as P

MESH = pl.DeviceIdType.MESH
LANES = 128
TILE = 256


def ladder_kernel(
    n, fold, left_hbm, right_hbm, amps_hbm, out_ref,
    left_in, amps_in, right_in, pick, left_rows, amps_f32, amps_rows, right_f32,
    integrals, total_buf, send_buf, recv_buf, left_sem, right_sem, amps_sem, send_sem, recv_sem,
):
    count_a, c_block, naux = left_hbm.shape
    _, count_b, width = right_hbm.shape
    pairs = amps_hbm.shape[0]
    chunks = width // LANES
    own_a = count_a // n
    me = lax.axis_index("row")

    q_tiles = naux // TILE
    m_halves = count_a * c_block // TILE

    def load_left(kt):
        lanes = pl.ds(kt * TILE, TILE)
        return pltpu.make_async_copy(
            left_hbm.at[:, :, lanes], left_in.at[:, :, lanes], left_sem.at[kt]
        )

    def load_right(k, kt):
        rows = pl.ds(kt * TILE, TILE)
        return pltpu.make_async_copy(
            right_hbm.at[rows, :, pl.ds(k * LANES, LANES)], right_in.at[k, rows],
            right_sem.at[k * q_tiles + kt],
        )

    load_amps = pltpu.make_async_copy(amps_hbm, amps_in, amps_sem)
    for kt in range(q_tiles):
        load_left(kt).start()
        load_right(0, kt).start()
    for k in range(1, chunks):
        for kt in range(q_tiles):
            load_right(k, kt).start()
        if k == 1:
            load_amps.start()

    barrier = pltpu.get_barrier_semaphore()

    @pl.loop(1, n)
    def _(k):
        pl.semaphore_signal(
            barrier, inc=1, device_id={"row": lax.rem(me + k, n)}, device_id_type=MESH
        )

    outer = TILE // c_block
    i = lax.broadcasted_iota(jnp.int32, (TILE, TILE), 0)
    j = lax.broadcasted_iota(jnp.int32, (TILE, TILE), 1)
    pick[...] = (j == (i % outer) * c_block + i // outer).astype(jnp.bfloat16)

    def move_left(moved, kt):
        lanes = pl.ds(kt * TILE, TILE)

        def push(m, staging):
            if m == 0:
                load_left(kt).wait()
            pltpu.matmul_push_rhs(
                left_in[pl.ds(m * outer, outer), :, lanes].reshape(TILE, TILE), staging, m
            )

        def multiply(m, staging):
            pltpu.matmul_acc_lhs(moved[m], pick[...], load_staged_rhs=staging)

        def finish():
            for m in range(2):
                left_rows[pl.ds(m * TILE, TILE), lanes] = pltpu.matmul_pop(moved[m]).astype(
                    jnp.bfloat16
                )

        return push, multiply, finish

    def stage_right(i):
        k, kt = divmod(i, q_tiles)
        load_right(k, kt).wait()
        flat = right_in.at[k].reshape(naux * count_b, LANES)
        right_f32[i % len(right_f32)][...] = flat[
            pl.ds(kt * TILE * count_b, TILE * count_b), :
        ].astype(jnp.float32)

    def split_amps(k, part, parts):
        lanes = pl.ds(k * LANES, LANES)
        staged = amps_f32[k % 2]
        if part == 0:
            if k == 0:
                load_amps.wait()
            staged[...] = amps_in[:, :, lanes].astype(jnp.float32).reshape(pairs * c_block, LANES)
        for c in range(part * c_block // parts, (part + 1) * c_block // parts):
            picked = staged[pl.ds(c, pairs, stride=c_block), :].astype(jnp.bfloat16)
            for f in range(fold):
                amps_rows[k % 2][
                    pl.ds(((c // 2) * fold + f) * pairs, pairs), pl.ds((c % 2) * LANES, LANES)
                ] = picked

    def block_of(k, g):
        return jnp.concatenate(
            [
                jnp.concatenate(
                    [
                        integrals[k % 2][
                            pl.ds(h * TILE + (g * 2 + e) * outer, outer), pl.ds(b * LANES, LANES)
                        ]
                        for e in range(2)
                    ],
                    axis=1,
                )
                for b in range(count_b)
                for h in range(m_halves)
            ],
            axis=0,
        )

    def integrate(acc, k, kt):
        def push(m, staging):
            rows = right_f32[(k * q_tiles + kt) % len(right_f32)]
            tile = [
                rows[pl.ds(m * (count_b // 2) + e, TILE, stride=count_b), :].astype(jnp.bfloat16)
                for e in range(count_b // 2)
            ]
            pltpu.matmul_push_rhs(jnp.concatenate(tile, axis=1), staging, m)

        def multiply(m, staging):
            for h in range(m_halves):
                pltpu.matmul_acc_lhs(
                    acc[m][h], left_rows[pl.ds(h * TILE, TILE), pl.ds(kt * TILE, TILE)],
                    load_staged_rhs=staging if h == 0 else None,
                )

        def finish():
            if kt == q_tiles - 1:
                for h in range(m_halves):
                    for m in range(2):
                        integrals[k % 2][pl.ds(h * TILE, TILE), pl.ds(m * TILE, TILE)] = (
                            pltpu.matmul_pop(acc[m][h]).astype(jnp.bfloat16)
                        )

        return push, multiply, finish

    def contract(acc_out, k, p):
        def push(m, staging):
            pltpu.matmul_push_rhs(
                amps_rows[k % 2][pl.ds((2 * p + m) * TILE, TILE), :], staging, m, transpose=True
            )

        def multiply(m, staging):
            for e in range(2):
                pltpu.matmul_acc_lhs(
                    acc_out[m][e], block_of(k, 2 * (2 * p + m) + e),
                    load_staged_rhs=staging if e == 0 else None,
                )

        return push, multiply, lambda: None

    def on_units(acc, acc_out, moved):
        tiles = [(move_left(moved, kt), None) for kt in range(2)]
        last = chunks * q_tiles
        half = q_tiles // 2
        for k in range(chunks):
            for kt in range(q_tiles):
                i = k * q_tiles + kt
                beside = []
                if i + 2 < last:
                    beside.append(functools.partial(stage_right, i + 2))
                if k > 0 and kt < half:
                    beside.append(functools.partial(split_amps, k - 1, kt, half))
                if k == chunks - 1 and kt >= half:
                    beside.append(functools.partial(split_amps, k, kt - half, q_tiles - half))
                tiles.append((integrate(acc, k, kt), beside))
                if i + 2 < q_tiles:
                    tiles.append((move_left(moved, i + 2), None))
                if k > 0 and kt in (half, half + 1):
                    tiles.append((contract(acc_out, k - 1, kt - half), []))
        tiles += [(contract(acc_out, chunks - 1, p), []) for p in range(2)]

        stage_right(0)
        stage_right(1)
        for m in range(2):
            tiles[0][0][0](m, 0)
        late = None
        for i, ((_, multiply, finish), beside) in enumerate(tiles):
            if i + 1 < len(tiles):
                for m in range(2):
                    tiles[i + 1][0][0](m, (i + 1) % 2)
            if late is not None and beside is None:
                late()
                late = None
            for m in range(2):
                multiply(m, i % 2)
            for run in beside or []:
                run()
            if late is not None:
                late()
            late = finish if beside is None else None
            if late is None:
                finish()
        total = 0.0
        for m in range(2):
            for e in range(2):
                total += pltpu.matmul_pop(acc_out[m][e])[:, e * LANES : (e + 1) * LANES]
        total_buf[...] = total

    pl.run_scoped(
        on_units,
        [[pltpu.ACC(m)((TILE, TILE), jnp.float32)] * m_halves for m in range(2)],
        [[pltpu.ACC(m)((count_a * count_b, TILE), jnp.float32)] * 2 for m in range(2)],
        [pltpu.ACC(m)((TILE, TILE), jnp.float32) for m in range(2)],
    )
    total = total_buf[...]

    lane = lax.broadcasted_iota(jnp.int32, (count_a, fold * pairs), 1)
    for g in range(count_b // fold):
        row = total[g * fold * count_a : (g * fold + 1) * count_a]
        for f in range(1, fold):
            b = g * fold + f
            row = jnp.where(lane >= f * pairs, total[b * count_a : (b + 1) * count_a], row)
        send_buf[:, g, :] = row

    pl.semaphore_wait(barrier, n - 1)

    @pl.loop(1, n)
    def _(k):
        to = lax.rem(me + k, n)
        pltpu.make_async_remote_copy(
            src_ref=send_buf.at[pl.ds(to * own_a, own_a)],
            dst_ref=recv_buf.at[pl.ds((k - 1) * own_a, own_a)],
            send_sem=send_sem,
            recv_sem=recv_sem,
            device_id={"row": to},
            device_id_type=MESH,
        ).start()

    every = recv_buf.at[pl.ds(0, (n - 1) * own_a)]
    pltpu.make_async_copy(every, every, recv_sem).wait()
    mine = send_buf[pl.ds(me * own_a, own_a)]
    got = recv_buf[...].reshape((n - 1, own_a) + recv_buf.shape[1:])
    result = mine + jnp.sum(got, axis=0)
    for b in range(count_b):
        out_ref[:, b, :] = result[:, b // fold, (b % fold) * pairs : (b % fold + 1) * pairs]
    pltpu.make_async_copy(every, every, send_sem).wait()


def per_device(n, left_factors, right_factors, amplitudes):
    left = lax.all_gather(left_factors, "col", axis=0, tiled=True)
    right = lax.all_gather(right_factors, "col", axis=0, tiled=True)
    naux, count_a, c_block = left.shape
    _, count_b, width = right.shape
    pairs = amplitudes.shape[0]
    fold = 2 if 2 * pairs == LANES and count_b % 2 == 0 else 1
    own_a = count_a // n
    anywhere = pl.BlockSpec(memory_space=pl.ANY)
    bf16, f32 = jnp.bfloat16, jnp.float32
    piece = (count_b // fold, fold * pairs)
    out = pl.pallas_call(
        functools.partial(ladder_kernel, n, fold),
        out_shape=jax.ShapeDtypeStruct((own_a, count_b, pairs), f32),
        in_specs=[anywhere] * 3,
        out_specs=pl.BlockSpec(memory_space=pltpu.VMEM),
        scratch_shapes=[
            pltpu.VMEM((count_a, c_block, naux), bf16),
            pltpu.VMEM((pairs, c_block, width), bf16),
            pltpu.VMEM((width // LANES, naux, count_b, LANES), bf16),
            pltpu.VMEM((TILE, TILE), bf16),
            pltpu.VMEM((c_block * count_a, naux), bf16),
            [pltpu.VMEM((pairs * c_block, LANES), f32)] * 2,
            [pltpu.VMEM((c_block // 2 * fold * pairs, TILE), bf16)] * 2,
            [pltpu.VMEM((TILE * count_b, LANES), f32)] * 4,
            [pltpu.VMEM((c_block * count_a, count_b * LANES), bf16)] * 2,
            pltpu.VMEM((count_b * count_a, fold * pairs), f32),
            pltpu.VMEM((count_a,) + piece, f32),
            pltpu.VMEM(((n - 1) * own_a,) + piece, f32),
            pltpu.SemaphoreType.DMA((naux // TILE,)),
            pltpu.SemaphoreType.DMA((naux // TILE * (width // LANES),)),
            pltpu.SemaphoreType.DMA,
            pltpu.SemaphoreType.DMA,
            pltpu.SemaphoreType.DMA,
        ],
        compiler_params=pltpu.CompilerParams(
            collective_id=0, has_side_effects=True, vmem_limit_bytes=53 * 1024 * 1024
        ),
        name="ladder",
    )(jnp.transpose(left, (1, 2, 0)), right, amplitudes)
    return jnp.transpose(out, (2, 0, 1))


def solution(mesh):
    placed = (P("col", None, "row"), P("col", None, None), P("col", "row", None))
    return jax.shard_map(
        functools.partial(per_device, mesh.shape["row"]),
        mesh=mesh, in_specs=placed, out_specs=P("col", "row", None), check_vma=False,
    )
```

```python
import functools

import jax
import jax.numpy as jnp
from jax import lax
from jax.experimental import pallas as pl
from jax.experimental.pallas import tpu as pltpu
from jax.sharding import PartitionSpec as P

MESH = pl.DeviceIdType.MESH
LANES = 128
TILE = 256


def ladder_kernel(
    n, fold, left_hbm, right_hbm, amps_hbm, out_ref,
    left_in, amps_in, right_in, left_f32, left_rows, amps_f32, amps_rows, right_f32,
    integrals, total_buf, send_buf, recv_buf, left_sem, right_sem, amps_sem, send_sem, recv_sem,
):
    count_a, c_block, naux = left_hbm.shape
    _, count_b, width = right_hbm.shape
    pairs = amps_hbm.shape[0]
    chunks = width // LANES
    own_a = count_a // n
    me = lax.axis_index("row")

    q_tiles = naux // TILE
    m_halves = count_a * c_block // TILE

    group = 2 if q_tiles % 2 == 0 else 1

    def load_left(p):
        lanes = pl.ds(p * group * TILE, group * TILE)
        return pltpu.make_async_copy(
            left_hbm.at[:, :, lanes], left_in.at[:, :, lanes], left_sem.at[p]
        )

    def load_right(k, p):
        rows = pl.ds(p * group * TILE, group * TILE) if k == 0 else slice(None)
        return pltpu.make_async_copy(
            right_hbm.at[rows, :, pl.ds(k * LANES, LANES)], right_in.at[k, rows],
            right_sem.at[p if k == 0 else q_tiles - 1 + k],
        )

    load_amps = pltpu.make_async_copy(amps_hbm, amps_in, amps_sem)
    for p in range(q_tiles // group):
        load_left(p).start()
        load_right(0, p).start()
    for k in range(1, chunks):
        load_right(k, 0).start()
        if k == 1:
            load_amps.start()

    barrier = pltpu.get_barrier_semaphore()

    @pl.loop(1, n)
    def _(k):
        pl.semaphore_signal(
            barrier, inc=1, device_id={"row": lax.rem(me + k, n)}, device_id_type=MESH
        )

    def split_left(kt):
        for e in range(TILE // LANES):
            lanes = pl.ds(kt * TILE + e * LANES, LANES)
            staged = left_f32[e]
            staged[...] = (
                left_in[:, :, lanes].astype(jnp.float32).reshape(count_a * c_block, LANES)
            )
            for c in range(c_block):
                left_rows[pl.ds(c * count_a, count_a), lanes] = staged[
                    pl.ds(c, count_a, stride=c_block), :
                ].astype(jnp.bfloat16)

    def stage_right(i):
        k, kt = divmod(i, q_tiles)
        if k == 0 and kt % group == 0:
            load_left(kt // group).wait()
            load_right(k, kt // group).wait()
        elif k > 0 and kt == 0:
            load_right(k, 0).wait()
        flat = right_in.at[k].reshape(naux * count_b, LANES)
        right_f32[i % len(right_f32)][...] = flat[
            pl.ds(kt * TILE * count_b, TILE * count_b), :
        ].astype(jnp.float32)

    def split_amps(k, part, parts):
        lanes = pl.ds(k * LANES, LANES)
        staged = amps_f32[k % 2]
        if part == 0:
            if k == 0:
                load_amps.wait()
            staged[...] = amps_in[:, :, lanes].astype(jnp.float32).reshape(pairs * c_block, LANES)
        for c in range(part * c_block // parts, (part + 1) * c_block // parts):
            picked = staged[pl.ds(c, pairs, stride=c_block), :].astype(jnp.bfloat16)
            for f in range(fold):
                amps_rows[k % 2][
                    pl.ds(((c // 2) * fold + f) * pairs, pairs), pl.ds((c % 2) * LANES, LANES)
                ] = picked

    def block_of(k, g):
        return jnp.concatenate(
            [
                jnp.concatenate(
                    [
                        integrals[k % 2][
                            pl.ds((g * 2 + e) * count_a, count_a), pl.ds(b * LANES, LANES)
                        ]
                        for e in range(2)
                    ],
                    axis=1,
                )
                for b in range(count_b)
            ],
            axis=0,
        )

    def integrate(acc, k, kt):
        def push(m, staging):
            rows = right_f32[(k * q_tiles + kt) % len(right_f32)]
            tile = [
                rows[pl.ds(m * (count_b // 2) + e, TILE, stride=count_b), :].astype(jnp.bfloat16)
                for e in range(count_b // 2)
            ]
            pltpu.matmul_push_rhs(jnp.concatenate(tile, axis=1), staging, m)

        def multiply(m, staging):
            for h in range(m_halves):
                pltpu.matmul_acc_lhs(
                    acc[m][h], left_rows[pl.ds(h * TILE, TILE), pl.ds(kt * TILE, TILE)],
                    load_staged_rhs=staging if h == 0 else None,
                )

        def finish():
            if kt == q_tiles - 1:
                for h in range(m_halves):
                    for m in range(2):
                        integrals[k % 2][pl.ds(h * TILE, TILE), pl.ds(m * TILE, TILE)] = (
                            pltpu.matmul_pop(acc[m][h]).astype(jnp.bfloat16)
                        )

        return push, multiply, finish

    def contract(acc_out, k, p):
        def push(m, staging):
            pltpu.matmul_push_rhs(
                amps_rows[k % 2][pl.ds((2 * p + m) * TILE, TILE), :], staging, m, transpose=True
            )

        def multiply(m, staging):
            for e in range(2):
                pltpu.matmul_acc_lhs(
                    acc_out[m][e], block_of(k, 2 * (2 * p + m) + e),
                    load_staged_rhs=staging if e == 0 else None,
                )

        return push, multiply, lambda: None

    def on_units(acc, acc_out):
        tiles = []
        last = chunks * q_tiles
        half = q_tiles // 2
        for k in range(chunks):
            for kt in range(q_tiles):
                i = k * q_tiles + kt
                beside = []
                if i + 1 < q_tiles:
                    beside.append(functools.partial(split_left, i + 1))
                if i + 2 < last:
                    beside.append(functools.partial(stage_right, i + 2))
                if k > 0 and kt < half:
                    beside.append(functools.partial(split_amps, k - 1, kt, half))
                if k == chunks - 1 and kt >= half:
                    beside.append(functools.partial(split_amps, k, kt - half, q_tiles - half))
                tiles.append((integrate(acc, k, kt), beside))
                if k > 0 and kt in (half, half + 1):
                    tiles.append((contract(acc_out, k - 1, kt - half), []))
        tiles += [(contract(acc_out, chunks - 1, p), []) for p in range(2)]

        stage_right(0)
        split_left(0)
        stage_right(1)
        for m in range(2):
            tiles[0][0][0](m, 0)
        for i, ((_, multiply, finish), beside) in enumerate(tiles):
            if i + 1 < len(tiles):
                for m in range(2):
                    tiles[i + 1][0][0](m, (i + 1) % 2)
            for m in range(2):
                multiply(m, i % 2)
            for run in beside:
                run()
            finish()
        total = 0.0
        for m in range(2):
            for e in range(2):
                total += pltpu.matmul_pop(acc_out[m][e])[:, e * LANES : (e + 1) * LANES]
        total_buf[...] = total

    pl.run_scoped(
        on_units,
        [[pltpu.ACC(m)((TILE, TILE), jnp.float32)] * m_halves for m in range(2)],
        [[pltpu.ACC(m)((count_a * count_b, TILE), jnp.float32)] * 2 for m in range(2)],
    )
    total = total_buf[...]

    lane = lax.broadcasted_iota(jnp.int32, (count_a, fold * pairs), 1)
    for g in range(count_b // fold):
        row = total[g * fold * count_a : (g * fold + 1) * count_a]
        for f in range(1, fold):
            b = g * fold + f
            row = jnp.where(lane >= f * pairs, total[b * count_a : (b + 1) * count_a], row)
        send_buf[:, g, :] = row

    pl.semaphore_wait(barrier, n - 1)

    @pl.loop(1, n)
    def _(k):
        to = lax.rem(me + k, n)
        pltpu.make_async_remote_copy(
            src_ref=send_buf.at[pl.ds(to * own_a, own_a)],
            dst_ref=recv_buf.at[pl.ds((k - 1) * own_a, own_a)],
            send_sem=send_sem,
            recv_sem=recv_sem,
            device_id={"row": to},
            device_id_type=MESH,
        ).start()

    every = recv_buf.at[pl.ds(0, (n - 1) * own_a)]
    pltpu.make_async_copy(every, every, recv_sem).wait()
    mine = send_buf[pl.ds(me * own_a, own_a)]
    got = recv_buf[...].reshape((n - 1, own_a) + recv_buf.shape[1:])
    result = mine + jnp.sum(got, axis=0)
    for b in range(count_b):
        out_ref[:, b, :] = result[:, b // fold, (b % fold) * pairs : (b % fold + 1) * pairs]
    pltpu.make_async_copy(every, every, send_sem).wait()


def per_device(n, left_factors, right_factors, amplitudes):
    left = lax.all_gather(left_factors, "col", axis=0, tiled=True)
    right = lax.all_gather(right_factors, "col", axis=0, tiled=True)
    naux, count_a, c_block = left.shape
    _, count_b, width = right.shape
    pairs = amplitudes.shape[0]
    fold = 2 if 2 * pairs == LANES and count_b % 2 == 0 else 1
    own_a = count_a // n
    anywhere = pl.BlockSpec(memory_space=pl.ANY)
    bf16, f32 = jnp.bfloat16, jnp.float32
    piece = (count_b // fold, fold * pairs)
    out = pl.pallas_call(
        functools.partial(ladder_kernel, n, fold),
        out_shape=jax.ShapeDtypeStruct((own_a, count_b, pairs), f32),
        in_specs=[anywhere] * 3,
        out_specs=pl.BlockSpec(memory_space=pltpu.VMEM),
        scratch_shapes=[
            pltpu.VMEM((count_a, c_block, naux), bf16),
            pltpu.VMEM((pairs, c_block, width), bf16),
            pltpu.VMEM((width // LANES, naux, count_b, LANES), bf16),
            [pltpu.VMEM((count_a * c_block, LANES), f32)] * 2,
            pltpu.VMEM((c_block * count_a, naux), bf16),
            [pltpu.VMEM((pairs * c_block, LANES), f32)] * 2,
            [pltpu.VMEM((c_block // 2 * fold * pairs, TILE), bf16)] * 2,
            [pltpu.VMEM((TILE * count_b, LANES), f32)] * 4,
            [pltpu.VMEM((c_block * count_a, count_b * LANES), bf16)] * 2,
            pltpu.VMEM((count_b * count_a, fold * pairs), f32),
            pltpu.VMEM((count_a,) + piece, f32),
            pltpu.VMEM(((n - 1) * own_a,) + piece, f32),
            pltpu.SemaphoreType.DMA((naux // TILE,)),
            pltpu.SemaphoreType.DMA((naux // TILE + width // LANES - 1,)),
            pltpu.SemaphoreType.DMA,
            pltpu.SemaphoreType.DMA,
            pltpu.SemaphoreType.DMA,
        ],
        compiler_params=pltpu.CompilerParams(
            collective_id=0, has_side_effects=True, vmem_limit_bytes=53 * 1024 * 1024
        ),
        name="ladder",
    )(jnp.transpose(left, (1, 2, 0)), right, amplitudes)
    return jnp.transpose(out, (2, 0, 1))


def solution(mesh):
    placed = (P("col", None, "row"), P("col", None, None), P("col", "row", None))
    return jax.shard_map(
        functools.partial(per_device, mesh.shape["row"]),
        mesh=mesh, in_specs=placed, out_specs=P("col", "row", None), check_vma=False,
    )
```
